32 devices in a mesh: tm: 4 (over y, core), dp: 8 (over z, x).
Axes of the slice: x: 2, y: 2, z: 4, core: 2. Of those that a mesh axis runs over, the one named last changes fastest.
Arguments:
- tokens: bfloat16 [8, 8, 64, 1152], P('dp', 'tm'), may hold values from -6 to 6
- clip_frames: int32 [8, 4], P('dp'), may hold values from 1 to 4, 8 in all within a row
- teacher_scores: float32 [8, 4, 8], P('dp'), may hold values from -4 to 4
- ln_gain: float32 [1152], replicated, may hold values from 0.25 to 1.75
- w_qkv: bfloat16 [1152, 3456], replicated, may hold values from -1 to 1
- w_out: bfloat16 [1152, 1152], replicated, may hold values from -0.1875 to 0.1875
- out_gain: float32 [1152], replicated, may hold values from 0.25 to 1.75
- reward_head: float32 [1152, 8], replicated, may hold values from -1.8856181 to 1.8856181
Outputs:
- scores: float32 [8, 4, 8], P('dp')
- grad_qkv: float32 [1152, 3456], P('dp')
- grad_out: float32 [1152, 1152], P('dp')
The draws below stay inside these ranges and needn't reach their ends.
Inputs may be any that keep to these rules, and one draw needn't show every extreme that they name: `clip_frames`: each row lists the lengths of 4 clips laid end to end over its 8 frames; the longest clip of every row has exactly 4 frames.
All inputs are finite; a program needn't handle non-finite values.
Results may differ from the reference program's by a relative error of at most 0.033.
Values may be sent and summed in bfloat16 or wider, within the bound.
A program may use at most 128 MiB of HBM per device.

```python
import math
import jax
import jax.numpy as jnp
import numpy as np
from jax import lax

D = 1152
HEADS = 16
HEAD_DIM = 72
POS = 64
WINDOW = 8
CLIPS = 4
REWARDS = 8
FRAMES = 8
ROWS = 8
MOST = 4
N_TM = 4


def draw_tokens(key, part):
    key = jax.random.fold_in(key, 11)
    first_key = jax.random.fold_in(key, 0)
    full_shape = (ROWS, FRAMES, POS, D)
    values = jax.random.normal(first_key, full_shape, jnp.float32)
    return jnp.clip(values, -6.0, 6.0).astype(jnp.bfloat16)


def draw_w_qkv(key, part):
    key = jax.random.fold_in(key, 12)
    split_keys = jax.random.split(key, 1)
    fan_scale = D ** (-0.5)
    values = jax.random.normal(split_keys[0], (D, 3 * D), jnp.float32) * fan_scale
    return jnp.clip(values, -1.0, 1.0).astype(jnp.bfloat16)


def levels(stream_key, dims, pieces, least, largest):
    loudness, own = 1.0, jax.random.fold_in(stream_key, 6)
    for axis_at, parts in pieces:
        draws = jnp.exp(jax.random.uniform(jax.random.fold_in(own, axis_at), (parts,), jnp.float32, least / len(pieces), largest / len(pieces)))
        loudness = loudness * jnp.repeat(draws, dims[axis_at] // parts).reshape([-1 if axis == axis_at else 1 for axis in range(len(dims))])
    return loudness


def profile(count, total, reach, slope):
    loads = [(1 << 20) // math.isqrt(grade ** slope) + 1 for grade in range(2, count + 1)]
    spare, given = total - reach - (count - 1), [1] * (count - 1)
    while spare > 0:
        movable = [i for i in range(count - 1) if given[i] < reach]
        whole, remaining = sum([loads[i] for i in movable]), spare
        for i in movable:
            extra = min(reach - given[i], max(1, remaining * loads[i] // whole), spare)
            given[i] = given[i] + extra
            spare = spare - extra
    return np.array([reach] + given)


def uneven_parts(rng, number_of, total, reach, lean):
    if number_of == 2:
        one = jax.random.randint(rng, (), max(1, total - reach), min(reach, total - 1) + 1)
        return jnp.stack([one, total - one])
    sizes = jnp.asarray(profile(number_of, total, reach, lean), jnp.int32)
    pairs = (number_of - 1) // 2
    source_of, receiver = sizes[1:1 + 2 * pairs:2], sizes[2:2 + 2 * pairs:2]
    room = jnp.minimum(source_of - 1, reach - receiver)
    shifted = jax.random.randint(jax.random.fold_in(rng, 1), (pairs,), 0, 1 << 20) % (room + 1)
    sizes = sizes.at[1:1 + 2 * pairs:2].set(source_of - shifted).at[2:2 + 2 * pairs:2].set(receiver + shifted)
    return sizes[jax.random.permutation(jax.random.fold_in(rng, 2), number_of)]


def noise(rng, extent, deviation, most, pieces=(), kind=jnp.bfloat16):
    drawn = deviation * jax.random.normal(rng, extent, jnp.float32)
    if pieces:
        drawn = drawn * levels(rng, extent, pieces, -0.22, 0.18)
    return jnp.clip(drawn, -most, most).astype(kind)


def setup_inputs(seed: int = 0) -> dict:
    key_of = jax.random.split(jax.random.key(seed), 9)
    tokens = draw_tokens(jax.random.fold_in(key_of[8], 71), 0)
    clip_frames = jax.vmap(lambda own: uneven_parts(own, CLIPS, FRAMES, MOST, 2))(jax.random.split(key_of[1], ROWS)).reshape((ROWS, CLIPS)).astype(jnp.int32)
    teacher_scores = noise(key_of[2], (ROWS, CLIPS, REWARDS), 1.0, 4.0, ((0, 8),), jnp.float32)
    ln_gain = jnp.clip(1.0 + 0.15 * jax.random.normal(key_of[3], (D,), jnp.float32), 0.25, 1.75)
    w_qkv = draw_w_qkv(jax.random.fold_in(key_of[8], 71), 0)
    w_out = noise(key_of[5], (D, D), D ** -0.5, 0.1875)
    out_gain = jnp.clip(1.0 + 0.15 * jax.random.normal(key_of[6], (D,), jnp.float32), 0.25, 1.75)
    reward_head = noise(key_of[7], (D, REWARDS), (16 * D ** -0.5), 1.8856181, (), jnp.float32)
    return {"tokens": tokens, "clip_frames": clip_frames, "teacher_scores": teacher_scores, "ln_gain": ln_gain, "w_qkv": w_qkv, "w_out": w_out, "out_gain": out_gain, "reward_head": reward_head}


norm_eps = 1e-06
highest = lax.Precision.HIGHEST

def rounded(values):
    return lax.optimization_barrier(values.astype(jnp.bfloat16)).astype(jnp.float32)

def layer_norm(values, gain_vector):
    centre = values - lax.optimization_barrier(jnp.mean(values, axis=-1, keepdims=True))
    inv_std = lax.rsqrt(lax.optimization_barrier(jnp.mean(centre * centre, axis=-1, keepdims=True)) + norm_eps)
    normal_form = centre * inv_std
    return (normal_form * gain_vector, normal_form, inv_std)

def frame_clip(lengths, frame_ids):
    clip_ends = jnp.cumsum(lengths)
    return lax.optimization_barrier(jnp.sum((clip_ends[None, :] <= frame_ids[:, None]).astype(jnp.int32), axis=1)).astype(jnp.int32)

def one_row(row_tokens, lengths, targets, ln_gain, w_qkv, w_out, out_gain, reward_head):
    frames = FRAMES
    model_width = D
    score_scale = 1.0 / math.sqrt(HEAD_DIM)
    behind = WINDOW // 2
    ahead = WINDOW - behind - 1
    inputs = row_tokens.astype(jnp.float32)
    normed_full, _, _ = layer_norm(inputs, ln_gain)
    normed = normed_full.astype(jnp.bfloat16)
    projected = jnp.dot(normed.reshape(frames * POS, model_width), w_qkv, preferred_element_type=jnp.float32)
    projected = rounded(projected).reshape(frames, POS, 3, HEADS, HEAD_DIM)
    queries = projected[:, :, 0]
    key_rows = projected[:, :, 1]
    value_rows = projected[:, :, 2]
    clip_ids = frame_clip(lengths, jnp.arange(frames, dtype=jnp.int32))
    padding = ((behind, ahead), (0, 0), (0, 0), (0, 0))
    key_pad = jnp.pad(key_rows, padding)
    value_pad = jnp.pad(value_rows, padding)
    clip_pad = jnp.pad(clip_ids, (behind, ahead), constant_values=-1)
    key_window = jnp.stack([key_pad[offset:offset + frames] for offset in range(WINDOW)])
    value_window = jnp.stack([value_pad[offset:offset + frames] for offset in range(WINDOW)])
    allowed = jnp.stack([clip_pad[offset:offset + frames] == clip_ids for offset in range(WINDOW)])[:, :, None, None]
    logits = jnp.einsum('fphe,wfphe->wfph', queries, key_window) * score_scale
    masked = jnp.where(allowed, logits, -1e+30)
    row_peak = lax.optimization_barrier(jnp.max(masked, axis=0))
    exp_terms = jnp.exp(masked - row_peak)
    weights = exp_terms / lax.optimization_barrier(jnp.sum(exp_terms, axis=0))
    weights_low = rounded(weights)
    attended = rounded(jnp.einsum('wfph,wfphe->fphe', weights_low, value_window)).reshape(frames, POS, model_width)
    attended_low = attended.astype(jnp.bfloat16)
    mixed = inputs + jnp.dot(attended_low.reshape(frames * POS, model_width), w_out, preferred_element_type=jnp.float32).reshape(frames, POS, model_width)
    final_norm, centred, inv_std = layer_norm(mixed, out_gain)
    per_token = jnp.dot(final_norm.reshape(frames * POS, model_width), reward_head, precision=highest)
    frame_sums = lax.optimization_barrier(jnp.sum(per_token.reshape(frames, POS, REWARDS), axis=1))
    onehot = (clip_ids[:, None] == jnp.arange(CLIPS, dtype=jnp.int32)[None, :]).astype(jnp.float32)
    clip_sums = jnp.dot(onehot.T, frame_sums, precision=highest)
    counts = lengths.astype(jnp.float32) * POS
    scores = clip_sums / counts[:, None]
    residue = (scores - targets) / ROWS
    frame_grad = jnp.dot(jnp.dot(onehot, residue, precision=highest), reward_head.T, precision=highest)
    scaled = frame_grad[:, None, :] * out_gain
    mixed_grad = (scaled - lax.optimization_barrier(jnp.mean(scaled, axis=-1, keepdims=True)) - centred * lax.optimization_barrier(jnp.mean(scaled * centred, axis=-1, keepdims=True))) * inv_std
    mixed_grad_low = mixed_grad.astype(jnp.bfloat16)
    attended_grad = jnp.dot(mixed_grad_low.reshape(frames * POS, model_width), w_out.T, preferred_element_type=jnp.float32)
    attended_grad = rounded(attended_grad).reshape(frames, POS, HEADS, HEAD_DIM)
    weight_grad = jnp.einsum('fphe,wfphe->wfph', attended_grad, value_window)
    logit_grad = rounded(weights * (weight_grad - lax.optimization_barrier(jnp.sum(weights * weight_grad, axis=0))))
    query_grad = jnp.einsum('wfph,wfphe->fphe', logit_grad, key_window) * score_scale
    key_terms = jnp.einsum('wfph,fphe->wfphe', logit_grad, queries) * score_scale
    value_terms = jnp.einsum('wfph,fphe->wfphe', weights_low, attended_grad)
    key_grad_pad = jnp.zeros((frames + WINDOW - 1, POS, HEADS, HEAD_DIM), jnp.float32)
    value_grad_pad = jnp.zeros((frames + WINDOW - 1, POS, HEADS, HEAD_DIM), jnp.float32)
    for offset in range(WINDOW):
        key_grad_pad = key_grad_pad.at[offset:offset + frames].add(key_terms[offset])
        value_grad_pad = value_grad_pad.at[offset:offset + frames].add(value_terms[offset])
    key_grad = key_grad_pad[behind:behind + frames]
    value_grad = value_grad_pad[behind:behind + frames]
    projected_grad = jnp.stack([query_grad, key_grad, value_grad], axis=2).reshape(frames, POS, 3 * model_width)
    projected_grad = rounded(projected_grad)
    normed_blocks = normed.astype(jnp.float32).reshape(N_TM, 2 * POS, model_width)
    grad_blocks = projected_grad.reshape(N_TM, 2 * POS, 3 * model_width)
    qkv_parts = rounded(jnp.einsum('mtd,mte->mde', normed_blocks, grad_blocks))
    part_qkv = lax.optimization_barrier(jnp.sum(qkv_parts, axis=0))
    attended_blocks = attended.reshape(N_TM, 2 * POS, model_width)
    mixed_blocks = mixed_grad_low.astype(jnp.float32).reshape(N_TM, 2 * POS, model_width)
    out_parts = rounded(jnp.einsum('mtd,mte->mde', attended_blocks, mixed_blocks))
    part_out = lax.optimization_barrier(jnp.sum(out_parts, axis=0))
    return (scores, part_qkv, part_out)

def reference(tokens, clip_frames, teacher_scores, ln_gain, w_qkv, w_out, out_gain, reward_head):

    def row_step(totals, row_inputs):
        row_tokens, lengths, targets = row_inputs
        scores, part_qkv, part_out = one_row(row_tokens, lengths, targets, ln_gain, w_qkv, w_out, out_gain, reward_head)
        return ((totals[0] + part_qkv, totals[1] + part_out), scores)
    initial = (jnp.zeros((D, 3 * D), jnp.float32), jnp.zeros((D, D), jnp.float32))
    totals, scores = lax.scan(row_step, initial, (tokens, clip_frames, teacher_scores))
    return (scores, totals[0], totals[1])
```

```python
import math

import jax
import jax.numpy as jnp
from jax import lax
from jax.experimental import pallas as pl
from jax.experimental.pallas import tpu as pltpu
from jax.sharding import PartitionSpec as P

HEADS = 16
HEAD_DIM = 72
WINDOW = 8
LANES = 128


norm_eps = 1e-06
highest = lax.Precision.HIGHEST
score_scale = 1.0 / math.sqrt(HEAD_DIM)


def swapped(block, axis, bit):
    route = [(i, i ^ (1 << bit)) for i in range(lax.axis_size(axis))]
    return lax.ppermute(block, axis, route)


def layer_norm(values, gain_vector):
    centre = values - jnp.mean(values, axis=-1, keepdims=True)
    inv_std = lax.rsqrt(jnp.mean(centre * centre, axis=-1, keepdims=True) + norm_eps)
    normal_form = centre * inv_std
    return (normal_form * gain_vector, normal_form, inv_std)


def dot_nt(left, right):
    return lax.dot_general(
        left, right, (((1,), (1,)), ((), ())), preferred_element_type=jnp.float32
    )


def dot_tn(left, right):
    return lax.dot_general(
        left, right, (((0,), (0,)), ((), ())), preferred_element_type=jnp.float32
    )


def head_lanes(head):
    first, last = head * HEAD_DIM, (head + 1) * HEAD_DIM
    start = first // LANES * LANES
    stop = -(-last // LANES) * LANES
    lane = lax.broadcasted_iota(jnp.int32, (1, stop - start), 1) + start
    return start, stop, (lane >= first) & (lane < last)


def forward_kernel(projected_ref, allowed_ref, attended_ref, weights_ref, total):
    width = attended_ref.shape[1]
    total[...] = jnp.zeros_like(total)
    allowed = allowed_ref[...] > 0
    for head in range(HEADS):
        start, stop, own = head_lanes(head)
        query = projected_ref[:, start:stop]
        key = projected_ref[:, width + start : width + stop]
        value = projected_ref[:, 2 * width + start : 2 * width + stop]
        query = jnp.where(own, query, jnp.zeros_like(query))
        logits = jnp.where(allowed, dot_nt(query, key) * score_scale, -1e30)
        terms = jnp.exp(logits - jnp.max(logits, axis=1, keepdims=True))
        weights = terms / jnp.sum(terms, axis=1, keepdims=True)
        weights_ref[head] = weights
        mixed = jnp.dot(weights.astype(jnp.bfloat16), value, preferred_element_type=jnp.float32)
        total[:, start:stop] += jnp.where(own, mixed, 0.0)
    attended_ref[...] = total[...].astype(jnp.bfloat16)


def backward_kernel(projected_ref, weights_ref, grad_ref, out_ref, total):
    width = grad_ref.shape[1]
    total[...] = jnp.zeros_like(total)
    for head in range(HEADS):
        start, stop, own = head_lanes(head)
        query = projected_ref[:, start:stop]
        key = projected_ref[:, width + start : width + stop]
        value = projected_ref[:, 2 * width + start : 2 * width + stop]
        grad = grad_ref[:, start:stop]
        grad = jnp.where(own, grad, jnp.zeros_like(grad))
        weights = weights_ref[head]
        weight_grad = dot_nt(grad, value)
        mean_grad = jnp.sum(weights * weight_grad, axis=1, keepdims=True)
        logit_grad = (weights * (weight_grad - mean_grad)).astype(jnp.bfloat16)
        query_grad = jnp.dot(logit_grad, key, preferred_element_type=jnp.float32)
        key_grad = dot_tn(logit_grad, query)
        value_grad = dot_tn(weights.astype(jnp.bfloat16), grad)
        total[:, start:stop] += jnp.where(own, query_grad * score_scale, 0.0)
        total[:, width + start : width + stop] += jnp.where(own, key_grad * score_scale, 0.0)
        total[:, 2 * width + start : 2 * width + stop] += value_grad
    out_ref[...] = total[...].astype(jnp.bfloat16)


def attend(projected, allowed):
    count, width = projected.shape[0], projected.shape[1] // 3
    return pl.pallas_call(
        forward_kernel,
        out_shape=(
            jax.ShapeDtypeStruct((count, width), jnp.bfloat16),
            jax.ShapeDtypeStruct((HEADS, count, count), jnp.float32),
        ),
        in_specs=[pl.BlockSpec(memory_space=pltpu.VMEM)] * 2,
        out_specs=[pl.BlockSpec(memory_space=pltpu.VMEM)] * 2,
        scratch_shapes=[pltpu.VMEM((count, width), jnp.float32)],
        compiler_params=pltpu.CompilerParams(vmem_limit_bytes=24 * 1024 * 1024),
    )(projected, allowed)


def attend_grad(projected, weights, attended_grad):
    return pl.pallas_call(
        backward_kernel,
        out_shape=jax.ShapeDtypeStruct(projected.shape, jnp.bfloat16),
        in_specs=[pl.BlockSpec(memory_space=pltpu.VMEM)] * 3,
        out_specs=pl.BlockSpec(memory_space=pltpu.VMEM),
        scratch_shapes=[pltpu.VMEM(projected.shape, jnp.float32)],
        compiler_params=pltpu.CompilerParams(vmem_limit_bytes=24 * 1024 * 1024),
    )(projected, weights, attended_grad)


def summed_blocks(normed, attended, grads):
    n_tm, n_dp = lax.axis_size("tm"), lax.axis_size("dp")
    me_tm, me_dp = lax.axis_index("tm"), lax.axis_index("dp")
    count, width = normed.shape
    rows = width // n_dp
    columns = grads.shape[1] // n_tm
    first_out = n_tm * 3 // 4
    order = me_dp ^ jnp.arange(n_dp, dtype=jnp.int32)

    def relative_rows(values):
        blocks = jnp.take(values.T.reshape(n_dp, rows, count), order, axis=0)
        return blocks.reshape(width, count)

    left_qkv, left_out = relative_rows(normed), relative_rows(attended)
    pieces = 3
    piece = columns // pieces
    bits_tm, bits_dp = n_tm.bit_length() - 1, n_dp.bit_length() - 1
    lead = [("tm", 1), ("dp", 0), ("dp", 1)]
    rest = [("dp", b) for b in range(2, bits_dp)] + [("tm", b) for b in range(2, bits_tm)]
    steps = [[("tm", 0)] + lead[i:] + lead[:i] + rest for i in range(pieces)]

    def product(part, number):
        block = me_tm ^ number
        left = jnp.where(block < first_out, left_qkv, left_out)
        right = lax.dynamic_slice(grads, (0, block * columns + part * piece), (count, piece))
        full = jnp.dot(left, right, preferred_element_type=jnp.float32)
        return full.astype(jnp.bfloat16).reshape(n_dp, rows, piece)

    held = [{} for _ in range(pieces)]
    numbers = [list(range(n_tm)) for _ in range(pieces)]
    for part in range(pieces):
        for number in sorted(range(n_tm), key=lambda r: (1 - (r & 1), r)):
            held[part][number] = product(part, number)
    for at in range(len(steps[0])):
        for part in range(pieces):
            axis, bit = steps[part][at]
            blocks = held[part]
            if axis == "tm":
                going = [r for r in blocks if (r >> bit) & 1]
                for r in going:
                    other = swapped(blocks.pop(r), "tm", bit)
                    kept = r ^ (1 << bit)
                    total = blocks[kept].astype(jnp.float32) + other.astype(jnp.float32)
                    blocks[kept] = total.astype(jnp.bfloat16)
            else:
                for r in blocks:
                    done = sum(1 for a, b in steps[part][:at] if a == "dp" and b < bit)
                    size = 1 << (bit - done)
                    rank = blocks[r].shape[0] // (2 * size)
                    pair = blocks[r].reshape(rank, 2, size, rows, piece)
                    kept = pair[:, 0].reshape(rank * size, rows, piece)
                    going = pair[:, 1].reshape(rank * size, rows, piece)
                    other = swapped(going, "dp", bit)
                    total = kept.astype(jnp.float32) + other.astype(jnp.float32)
                    blocks[r] = total.astype(jnp.bfloat16)
    mine = jnp.concatenate([held[part][0][0] for part in range(pieces)], axis=1)
    gathered = mine[None]
    for bit in reversed(range(bits_tm)):
        gathered = jnp.concatenate([gathered, swapped(gathered, "tm", bit)], axis=0)
    place = []
    for number in range(n_tm):
        place.append(sum(((number >> b) & 1) << (bits_tm - 1 - b) for b in range(bits_tm)))
    place = jnp.array(place, dtype=jnp.int32)
    whole = []
    for block in range(n_tm):
        whole.append(lax.dynamic_index_in_dim(gathered, place[me_tm ^ block], 0, keepdims=False))
    qkv = jnp.concatenate(whole[:first_out], axis=1).astype(jnp.float32)
    out = jnp.concatenate(whole[first_out:], axis=1).astype(jnp.float32)
    return qkv, out


def on_device(tokens, clip_frames, teacher_scores, ln_gain, w_qkv, w_out, out_gain, reward_head):
    width = tokens.shape[3]
    n_tm = lax.axis_size("tm")
    row_count = lax.axis_size("dp")
    positions = tokens.shape[2]
    inputs = lax.all_to_all(tokens[0], "tm", split_axis=1, concat_axis=0, tiled=True)
    frames, own_positions = inputs.shape[0], inputs.shape[1]
    count = frames * own_positions
    inputs = inputs.reshape(count, width).astype(jnp.float32)
    lengths = clip_frames[0]
    index = jnp.arange(count, dtype=jnp.int32)
    frame, position = index // own_positions, index % own_positions
    clip = jnp.sum((jnp.cumsum(lengths)[None, :] <= frame[:, None]).astype(jnp.int32), axis=1)
    lag = frame[None, :] - frame[:, None]
    behind = WINDOW // 2
    allowed = (
        (position[None, :] == position[:, None])
        & (clip[None, :] == clip[:, None])
        & (lag >= -behind)
        & (lag < WINDOW - behind)
    )
    normed_full, _, _ = layer_norm(inputs, ln_gain)
    normed = normed_full.astype(jnp.bfloat16)
    projected = jnp.dot(normed, w_qkv, preferred_element_type=jnp.float32).astype(jnp.bfloat16)
    attended, weights = attend(projected, allowed.astype(jnp.float32))
    mixed = inputs + jnp.dot(attended, w_out, preferred_element_type=jnp.float32)
    final_norm, centred, inv_std = layer_norm(mixed, out_gain)
    per_token = jnp.dot(final_norm, reward_head, precision=highest)
    onehot = (clip[:, None] == jnp.arange(lengths.shape[0], dtype=jnp.int32)[None, :]).astype(
        jnp.float32
    )
    clip_totals = jnp.dot(onehot.T, per_token, precision=highest)
    for bit in range(n_tm.bit_length() - 1):
        clip_totals = clip_totals + swapped(clip_totals, "tm", bit)
    counts = lengths.astype(jnp.float32) * positions
    scores = clip_totals / counts[:, None]
    residue = (scores - teacher_scores[0]) / row_count
    clip_grad = jnp.dot(residue, reward_head.T, precision=highest) * out_gain
    scaled = jnp.dot(onehot, clip_grad, precision=highest)
    mixed_grad = (
        scaled
        - jnp.mean(scaled, axis=-1, keepdims=True)
        - centred * jnp.mean(scaled * centred, axis=-1, keepdims=True)
    ) * inv_std
    mixed_grad = mixed_grad.astype(jnp.bfloat16)
    attended_grad = dot_nt(mixed_grad, w_out).astype(jnp.bfloat16)
    projected_grad = attend_grad(projected, weights, attended_grad)
    grads = jnp.concatenate([projected_grad, mixed_grad], axis=1)
    qkv_total, out_total = summed_blocks(normed, attended, grads)
    return (scores[None], qkv_total, out_total)


def solution(mesh):
    return jax.shard_map(
        on_device,
        mesh=mesh,
        in_specs=(
            P("dp", "tm", None, None),
            P("dp", None),
            P("dp", None, None),
            P(),
            P(),
            P(),
            P(),
            P(),
        ),
        out_specs=(P("dp", None, None), P("dp", None), P("dp", None)),
        check_vma=False,
    )
```

```python
import math

import jax
import jax.numpy as jnp
from jax import lax
from jax.experimental import pallas as pl
from jax.experimental.pallas import tpu as pltpu
from jax.sharding import PartitionSpec as P

HEADS = 16
HEAD_DIM = 72
WINDOW = 8
LANES = 128


norm_eps = 1e-06
highest = lax.Precision.HIGHEST
score_scale = 1.0 / math.sqrt(HEAD_DIM)


def swapped(block, axis, bit):
    route = [(i, i ^ (1 << bit)) for i in range(lax.axis_size(axis))]
    return lax.ppermute(block, axis, route)


def layer_norm(values, gain_vector):
    centre = values - jnp.mean(values, axis=-1, keepdims=True)
    inv_std = lax.rsqrt(jnp.mean(centre * centre, axis=-1, keepdims=True) + norm_eps)
    normal_form = centre * inv_std
    return (normal_form * gain_vector, normal_form, inv_std)


def dot_nt(left, right):
    return lax.dot_general(
        left, right, (((1,), (1,)), ((), ())), preferred_element_type=jnp.float32
    )


def dot_tn(left, right):
    return lax.dot_general(
        left, right, (((0,), (0,)), ((), ())), preferred_element_type=jnp.float32
    )


def head_lanes(head):
    first, last = head * HEAD_DIM, (head + 1) * HEAD_DIM
    start = first // LANES * LANES
    stop = -(-last // LANES) * LANES
    lane = lax.broadcasted_iota(jnp.int32, (1, stop - start), 1) + start
    return start, stop, (lane >= first) & (lane < last)


def forward_kernel(projected_ref, allowed_ref, attended_ref, weights_ref, total):
    width = attended_ref.shape[1]
    total[...] = jnp.zeros_like(total)
    allowed = allowed_ref[...] > 0
    for head in range(HEADS):
        start, stop, own = head_lanes(head)
        query = projected_ref[:, start:stop]
        key = projected_ref[:, width + start : width + stop]
        value = projected_ref[:, 2 * width + start : 2 * width + stop]
        query = jnp.where(own, query, jnp.zeros_like(query))
        logits = jnp.where(allowed, dot_nt(query, key) * score_scale, -1e30)
        terms = jnp.exp(logits - jnp.max(logits, axis=1, keepdims=True))
        weights = terms / jnp.sum(terms, axis=1, keepdims=True)
        weights_ref[head] = weights
        mixed = jnp.dot(weights.astype(jnp.bfloat16), value, preferred_element_type=jnp.float32)
        total[:, start:stop] += jnp.where(own, mixed, 0.0)
    attended_ref[...] = total[...].astype(jnp.bfloat16)


def backward_kernel(projected_ref, weights_ref, grad_ref, out_ref, total):
    width = grad_ref.shape[1]
    total[...] = jnp.zeros_like(total)
    for head in range(HEADS):
        start, stop, own = head_lanes(head)
        query = projected_ref[:, start:stop]
        key = projected_ref[:, width + start : width + stop]
        value = projected_ref[:, 2 * width + start : 2 * width + stop]
        grad = grad_ref[:, start:stop]
        grad = jnp.where(own, grad, jnp.zeros_like(grad))
        weights = weights_ref[head]
        weight_grad = dot_nt(grad, value)
        mean_grad = jnp.sum(weights * weight_grad, axis=1, keepdims=True)
        logit_grad = (weights * (weight_grad - mean_grad)).astype(jnp.bfloat16)
        query_grad = jnp.dot(logit_grad, key, preferred_element_type=jnp.float32)
        key_grad = dot_tn(logit_grad, query)
        value_grad = dot_tn(weights.astype(jnp.bfloat16), grad)
        total[:, start:stop] += jnp.where(own, query_grad * score_scale, 0.0)
        total[:, width + start : width + stop] += jnp.where(own, key_grad * score_scale, 0.0)
        total[:, 2 * width + start : 2 * width + stop] += value_grad
    out_ref[...] = total[...].astype(jnp.bfloat16)


def attend(projected, allowed):
    count, width = projected.shape[0], projected.shape[1] // 3
    return pl.pallas_call(
        forward_kernel,
        out_shape=(
            jax.ShapeDtypeStruct((count, width), jnp.bfloat16),
            jax.ShapeDtypeStruct((HEADS, count, count), jnp.float32),
        ),
        in_specs=[pl.BlockSpec(memory_space=pltpu.VMEM)] * 2,
        out_specs=[pl.BlockSpec(memory_space=pltpu.VMEM)] * 2,
        scratch_shapes=[pltpu.VMEM((count, width), jnp.float32)],
        compiler_params=pltpu.CompilerParams(vmem_limit_bytes=24 * 1024 * 1024),
    )(projected, allowed)


def attend_grad(projected, weights, attended_grad):
    return pl.pallas_call(
        backward_kernel,
        out_shape=jax.ShapeDtypeStruct(projected.shape, jnp.bfloat16),
        in_specs=[pl.BlockSpec(memory_space=pltpu.VMEM)] * 3,
        out_specs=pl.BlockSpec(memory_space=pltpu.VMEM),
        scratch_shapes=[pltpu.VMEM(projected.shape, jnp.float32)],
        compiler_params=pltpu.CompilerParams(vmem_limit_bytes=24 * 1024 * 1024),
    )(projected, weights, attended_grad)


def summed_blocks(normed, attended, grads):
    n_tm, n_dp = lax.axis_size("tm"), lax.axis_size("dp")
    me_tm, me_dp = lax.axis_index("tm"), lax.axis_index("dp")
    count, width = normed.shape
    rows = width // n_dp
    columns = grads.shape[1] // n_tm
    first_out = n_tm * 3 // 4
    row = jnp.arange(width, dtype=jnp.int32)
    source = (row // rows ^ me_dp) * rows + row % rows
    places = (source[:, None] == row[None, :]).astype(jnp.bfloat16)
    left_qkv = dot_nt(places, normed).astype(jnp.bfloat16)
    left_out = dot_nt(places, attended).astype(jnp.bfloat16)
    pieces = 3
    piece = columns // pieces
    bits_tm, bits_dp = n_tm.bit_length() - 1, n_dp.bit_length() - 1
    lead = [("tm", 1), ("dp", 0), ("dp", 1)]
    rest = [("dp", b) for b in range(2, bits_dp)] + [("tm", b) for b in range(2, bits_tm)]
    steps = [[("tm", 0)] + lead[i:] + lead[:i] + rest for i in range(pieces)]

    def product(part, number):
        block = me_tm ^ number
        left = jnp.where(block < first_out, left_qkv, left_out)
        right = lax.dynamic_slice(grads, (0, block * columns + part * piece), (count, piece))
        full = jnp.dot(left, right, preferred_element_type=jnp.float32)
        return full.astype(jnp.bfloat16).reshape(n_dp, rows, piece)

    held = [{} for _ in range(pieces)]
    numbers = [list(range(n_tm)) for _ in range(pieces)]
    for part in range(pieces):
        for number in sorted(range(n_tm), key=lambda r: (1 - (r & 1), r)):
            held[part][number] = product(part, number)
    def halves(part, at):
        axis, bit = steps[part][at]
        blocks = held[part]
        if axis == "tm":
            kept = {r: blocks[r] for r in blocks if not (r >> bit) & 1}
            return kept, {r: blocks[r ^ (1 << bit)] for r in kept}
        done = sum(1 for a, b in steps[part][:at] if a == "dp" and b < bit)
        size = 1 << (bit - done)
        kept, going = {}, {}
        for r in blocks:
            pair = blocks[r].reshape(-1, 2, size, rows, piece)
            kept[r] = pair[:, 0].reshape(-1, rows, piece)
            going[r] = pair[:, 1].reshape(-1, rows, piece)
        return kept, going

    for at in range(len(steps[0])):
        split = [halves(part, at) for part in range(pieces)]
        if at == 0:
            sends = [[going[r] for r in going] for _, going in split]
        else:
            sends = [[jnp.concatenate([going[r] for r in going], axis=0)] for _, going in split]
            sends = lax.optimization_barrier(sends)
        for part in range(pieces):
            kept = split[part][0]
            came = [swapped(block, *steps[part][at]) for block in sends[part]]
            if len(came) < len(kept):
                came = jnp.split(came[0], len(kept), axis=0)
            for r, other in zip(kept, came):
                total = kept[r].astype(jnp.float32) + other.astype(jnp.float32)
                kept[r] = total.astype(jnp.bfloat16)
            held[part] = kept
    mine = jnp.concatenate([held[part][0][0] for part in range(pieces)], axis=1)
    gathered = {0: mine}
    for bit in list(range(1, bits_tm))[::-1] + [0]:
        for r in list(gathered):
            gathered[r ^ (1 << bit)] = swapped(gathered[r], "tm", bit)
    whole = [gathered[r] for r in range(n_tm)]
    for bit in range(bits_tm):
        odd = (me_tm >> bit) & 1 == 1
        whole = [jnp.where(odd, whole[r ^ (1 << bit)], whole[r]) for r in range(n_tm)]
    qkv = jnp.concatenate(whole[:first_out], axis=1).astype(jnp.float32)
    out = jnp.concatenate(whole[first_out:], axis=1).astype(jnp.float32)
    return qkv, out


def on_device(tokens, clip_frames, teacher_scores, ln_gain, w_qkv, w_out, out_gain, reward_head):
    width = tokens.shape[3]
    n_tm = lax.axis_size("tm")
    row_count = lax.axis_size("dp")
    positions = tokens.shape[2]
    inputs = lax.all_to_all(tokens[0], "tm", split_axis=1, concat_axis=0, tiled=True)
    frames, own_positions = inputs.shape[0], inputs.shape[1]
    count = frames * own_positions
    inputs = inputs.reshape(count, width).astype(jnp.float32)
    lengths = clip_frames[0]
    index = jnp.arange(count, dtype=jnp.int32)
    frame, position = index // own_positions, index % own_positions
    clip = jnp.sum((jnp.cumsum(lengths)[None, :] <= frame[:, None]).astype(jnp.int32), axis=1)
    lag = frame[None, :] - frame[:, None]
    behind = WINDOW // 2
    allowed = (
        (position[None, :] == position[:, None])
        & (clip[None, :] == clip[:, None])
        & (lag >= -behind)
        & (lag < WINDOW - behind)
    )
    normed_full, _, _ = layer_norm(inputs, ln_gain)
    normed = normed_full.astype(jnp.bfloat16)
    projected = jnp.dot(normed, w_qkv, preferred_element_type=jnp.float32).astype(jnp.bfloat16)
    attended, weights = attend(projected, allowed.astype(jnp.float32))
    mixed = inputs + jnp.dot(attended, w_out, preferred_element_type=jnp.float32)
    final_norm, centred, inv_std = layer_norm(mixed, out_gain)
    per_token = jnp.dot(final_norm, reward_head, precision=highest)
    onehot = (clip[:, None] == jnp.arange(lengths.shape[0], dtype=jnp.int32)[None, :]).astype(
        jnp.float32
    )
    clip_totals = jnp.dot(onehot.T, per_token, precision=highest)
    for bit in range(n_tm.bit_length() - 1):
        clip_totals = clip_totals + swapped(clip_totals, "tm", bit)
    counts = lengths.astype(jnp.float32) * positions
    scores = clip_totals / counts[:, None]
    residue = (scores - teacher_scores[0]) / row_count
    clip_grad = jnp.dot(residue, reward_head.T, precision=highest) * out_gain
    scaled = jnp.dot(onehot, clip_grad, precision=highest)
    mixed_grad = (
        scaled
        - jnp.mean(scaled, axis=-1, keepdims=True)
        - centred * jnp.mean(scaled * centred, axis=-1, keepdims=True)
    ) * inv_std
    mixed_grad = mixed_grad.astype(jnp.bfloat16)
    attended_grad = dot_nt(mixed_grad, w_out).astype(jnp.bfloat16)
    projected_grad = attend_grad(projected, weights, attended_grad)
    grads = jnp.concatenate([projected_grad, mixed_grad], axis=1)
    qkv_total, out_total = summed_blocks(normed, attended, grads)
    return (scores[None], qkv_total, out_total)


def solution(mesh):
    return jax.shard_map(
        on_device,
        mesh=mesh,
        in_specs=(
            P("dp", "tm", None, None),
            P("dp", None),
            P("dp", None, None),
            P(),
            P(),
            P(),
            P(),
            P(),
        ),
        out_specs=(P("dp", None, None), P("dp", None), P("dp", None)),
        check_vma=False,
    )
```
